512 devices in a mesh: replica: 32 (over x_hi, z), fsdp: 16 (over y, x_lo, core).
Axes of the slice: x: 4 (x_hi: 2, x_lo: 2; x = x_hi * 2 + x_lo), y: 4, z: 16, core: 2. Of those that a mesh axis runs over, the one named last changes fastest.
Arguments:
- activations: bfloat16 [32, 2048, 4096], P('replica', 'fsdp'), may hold values from -6 to 6
- cotangent: bfloat16 [32, 2048, 512], P('replica', 'fsdp'), may hold values from -6 to 6
- master: float32 [32, 4096, 512], P('replica', 'fsdp'), may hold values from -6 to 6
- moment_one: float32 [32, 4096, 512], P('replica', 'fsdp'), may hold values from -4 to 4
- moment_two: float32 [32, 4096, 512], P('replica', 'fsdp'), may hold values from 0.001 to 1
- lengths: int32 [32, 16], P('replica'), may hold values from 1 to 128, 1536 in all within a row
- pseudo_grad: float32 [32, 16, 256, 512], P('replica', 'fsdp'), may hold values from -8 to 8
- anchor: float32 [16, 256, 512], P('fsdp', 'replica'), may hold values from -6 to 6
- momentum: float32 [16, 256, 512], P('fsdp', 'replica'), may hold values from -4 to 4
Outputs:
- input_grad: bfloat16 [32, 2048, 4096], P('replica', 'fsdp')
- master_out: float32 [32, 4096, 512], P('replica', 'fsdp')
- fragment_weights: bfloat16 [16, 256, 512], P('fsdp')
- anchor_out: float32 [16, 256, 512], P('fsdp', 'replica')
- momentum_out: float32 [16, 256, 512], P('fsdp', 'replica')
The draws below stay inside these ranges and needn't reach their ends.
Inputs may be any that keep to these rules, and one draw needn't show every extreme that they name: In each replica the 16 lengths sum to 1536 and one of them is exactly 128.
All inputs are finite; a program needn't handle non-finite values.
Results may differ from the reference program's by a relative error of at most 0.02.
Values may be sent and summed in bfloat16 or wider, within the bound.
No kernel may reach another device: no remote copies, remote signals or barrier semaphores. Data moves between devices by JAX's collectives and lax.ppermute only.
A program may use at most 64 MiB of HBM per device.

```python
import math
import jax
import jax.numpy as jnp
import numpy as np
from jax import lax

DW = 4096
KVW = 512
TOK_DEV = 128
REPLICAS = 32
FSDP_SHARDS = 16
TOKENS = 2048
SHARD_ROWS = 256


def spiked(array, own_key, source, target, parts, factor):
    owner, partner = [(jnp.arange(array.shape[dim]) // (array.shape[dim] // parts)).reshape([-1 if axis == dim else 1 for axis in range(array.ndim)]) for dim in (source, target)]
    chosen = jax.random.permutation(own_key, parts)[partner]
    strong = (owner == chosen) | (owner == (partner + parts // 2) % parts)
    return jnp.where(strong, factor * array, array)


def shard_levels(stream_key, extent, pieces, smallest, largest):
    factor_of, own = 1.0, jax.random.fold_in(stream_key, 6)
    for dim, shards_of in pieces:
        draws = jnp.exp(jax.random.uniform(jax.random.fold_in(own, dim), (shards_of,), jnp.float32, smallest / len(pieces), largest / len(pieces)))
        factor_of = factor_of * jnp.repeat(draws, extent[dim] // shards_of).reshape([-1 if axis == dim else 1 for axis in range(len(extent))])
    return factor_of


def profile(count, total, most, skew):
    loads = [(1 << 20) // math.isqrt(rank ** skew) + 1 for rank in range(2, count + 1)]
    rest, counts = total - most - (count - 1), [1] * (count - 1)
    while rest > 0:
        movable = [i for i in range(count - 1) if counts[i] < most]
        whole, budget = sum([loads[i] for i in movable]), rest
        for i in movable:
            addition = min(most - counts[i], max(1, budget * loads[i] // whole), rest)
            counts[i] = counts[i] + addition
            rest = rest - addition
    return np.array([most] + counts)


def ragged(rng, number_of, total, reach, skew):
    if number_of == 2:
        one = jax.random.randint(rng, (), max(1, total - reach), min(reach, total - 1) + 1)
        return jnp.stack([one, total - one])
    sizes = jnp.asarray(profile(number_of, total, reach, skew), jnp.int32)
    twos = (number_of - 1) // 2
    source_of, sink = sizes[1:1 + 2 * twos:2], sizes[2:2 + 2 * twos:2]
    margin = jnp.minimum(source_of - 1, reach - sink)
    shifted = jax.random.randint(jax.random.fold_in(rng, 1), (twos,), 0, 1 << 20) % (margin + 1)
    sizes = sizes.at[1:1 + 2 * twos:2].set(source_of - shifted).at[2:2 + 2 * twos:2].set(sink + shifted)
    return sizes[jax.random.permutation(jax.random.fold_in(rng, 2), number_of)]


def noise(rng, extent, spread, reach, split=(), kind=jnp.bfloat16):
    loudness = shard_levels(rng, extent, split, -0.22, 0.18) if split else 1.0
    result = jax.random.normal(rng, extent, jnp.float32) * spread * loudness
    return jnp.minimum(jnp.maximum(result, -reach), reach).astype(kind)


def gaussian_with(rng, dims, scale, reach, pieces, heavy, kind=jnp.bfloat16):
    values = scale * jax.random.normal(rng, dims, jnp.float32)
    if pieces:
        values = values * shard_levels(rng, dims, pieces, -0.22, 0.18)
    return jnp.clip(spiked(values, jax.random.fold_in(rng, 3), *heavy), -reach, reach).astype(kind)


def setup_inputs(seed: int = 0) -> dict:
    seeds = jax.random.split(jax.random.key(seed), 10)
    activations = gaussian_with(seeds[0], (REPLICAS, TOKENS, DW), 1.0, 6.0, ((0, 32), (1, 16)), (1, 2, 16, 2.0))
    cotangent = noise(seeds[1], (REPLICAS, TOKENS, KVW), 1.0, 6.0, ((0, 32), (1, 16)))
    master = noise(seeds[2], (REPLICAS, DW, KVW), 1.0, 6.0, ((0, 32), (1, 16)), jnp.float32)
    moment_one = noise(seeds[3], (REPLICAS, DW, KVW), 0.3, 4.0, ((0, 32), (1, 16)), jnp.float32)
    moment_two = jnp.clip(jnp.exp(math.log(1.0) - 6.9077552 * jax.random.uniform(seeds[4], (REPLICAS, DW, KVW), jnp.float32) ** shard_levels(seeds[4], (REPLICAS, DW, KVW), ((0, 32), (1, 16)), -0.2, 0.2)), 0.001, 1.0)
    lengths = jax.vmap(lambda own: ragged(own, FSDP_SHARDS, 3 * TOKENS // 4, TOK_DEV, 2))(jax.random.split(seeds[5], REPLICAS)).reshape((REPLICAS, FSDP_SHARDS)).astype(jnp.int32)
    pseudo_grad = gaussian_with(seeds[6], (REPLICAS, FSDP_SHARDS, SHARD_ROWS, KVW), 1.0, 8.0, ((0, 32), (1, 16)), (0, 2, 32, 2.75), jnp.float32)
    anchor = noise(seeds[7], (FSDP_SHARDS, SHARD_ROWS, KVW), 1.0, 6.0, ((0, 16), (1, 32)), jnp.float32)
    momentum = noise(seeds[8], (FSDP_SHARDS, SHARD_ROWS, KVW), 0.3, 4.0, ((0, 16), (1, 32)), jnp.float32)
    return {"activations": activations, "cotangent": cotangent, "master": master, "moment_one": moment_one, "moment_two": moment_two, "lengths": lengths, "pseudo_grad": pseudo_grad, "anchor": anchor, "momentum": momentum}


def replica_step(activations, cotangent, master, moment_one, moment_two, lengths):
    slot = jnp.arange(TOKENS) % TOK_DEV
    owner = jnp.arange(TOKENS) // TOK_DEV
    alive = slot < lengths[owner]
    masked = jnp.where(alive[:, None], cotangent, jnp.zeros((), cotangent.dtype))
    weights_half = master.astype(jnp.bfloat16)
    factor = 1.0 / math.sqrt(DW)
    input_grad = (jnp.dot(masked, weights_half.T, preferred_element_type=jnp.float32) * factor).astype(jnp.bfloat16)

    def add_block(running, blocks):
        act_block, cot_block = blocks
        partial_value = jnp.dot(act_block.T, cot_block, preferred_element_type=jnp.float32)
        rounded = lax.optimization_barrier(partial_value.astype(jnp.bfloat16))
        return (running + rounded.astype(jnp.float32), None)
    start_sum = jnp.zeros((DW, KVW), jnp.float32)
    summed, _ = lax.scan(add_block, start_sum, (activations.reshape(FSDP_SHARDS, TOK_DEV, DW), masked.reshape(FSDP_SHARDS, TOK_DEV, KVW)))
    grad = summed * factor
    first = 0.9 * moment_one + 0.1 * grad
    second = 0.95 * moment_two + 0.05 * grad * grad
    master_out = master * (1.0 - 0.1 * 0.1) - 0.1 * first / (jnp.sqrt(second) + 1e-08)
    return (input_grad, master_out)

def reference(activations, cotangent, master, moment_one, moment_two, lengths, pseudo_grad, anchor, momentum):

    def one_replica(inputs):
        return replica_step(*inputs)
    input_grad, master_out = lax.map(one_replica, (activations, cotangent, master, moment_one, moment_two, lengths))
    delta = lax.optimization_barrier(jnp.sum(pseudo_grad, axis=0)) / REPLICAS
    momentum_out = 0.9 * momentum + delta
    anchor_out = anchor - 0.7 * (delta + 0.9 * momentum_out)
    return (input_grad, master_out, anchor_out.astype(jnp.bfloat16), anchor_out, momentum_out)
```

```python
import math

import jax
import jax.numpy as jnp
from jax import lax
from jax.sharding import PartitionSpec as P


def local(
    activations, cotangent, master, moment_one, moment_two, lengths, pseudo_grad, anchor, momentum
):
    shards = lax.axis_size("fsdp")
    replicas = lax.axis_size("replica")
    fsdp_index = lax.axis_index("fsdp")
    tok_count = activations.shape[1]
    width = activations.shape[2]
    share_rows = anchor.shape[1]
    factor = 1.0 / math.sqrt(width)

    pieces = pseudo_grad[0, 0].astype(jnp.bfloat16).reshape(replicas, share_rows, -1)
    pieces = lax.all_to_all(pieces, "replica", 0, 0)
    delta = jnp.sum(pieces.astype(jnp.float32), axis=0) / replicas
    momentum_out = 0.9 * momentum[0] + delta
    anchor_out = anchor[0] - 0.7 * (delta + 0.9 * momentum_out)
    fresh = jnp.broadcast_to(anchor_out.astype(jnp.bfloat16)[None], pieces.shape)
    fresh = lax.all_to_all(fresh, "replica", 0, 0).reshape(pseudo_grad.shape[2:])

    own_length = lax.dynamic_index_in_dim(lengths[0], fsdp_index, keepdims=False)
    alive = jnp.arange(tok_count) < own_length
    masked = jnp.where(alive[:, None], cotangent[0], jnp.zeros((), cotangent.dtype))
    weights = lax.all_gather(master[0].astype(jnp.bfloat16), "fsdp", axis=0, tiled=True)
    everyone = lax.all_gather(masked, "fsdp", axis=0, tiled=True)

    features = lax.all_to_all(activations[0], "fsdp", 1, 0, tiled=True)
    summed = lax.dot_general(
        features, everyone, (((0,), (0,)), ((), ())), preferred_element_type=jnp.float32
    )
    grad = summed * factor
    first = 0.9 * moment_one[0] + 0.1 * grad
    second = 0.95 * moment_two[0] + 0.05 * grad * grad
    master_out = master[0] * (1.0 - 0.1 * 0.1) - 0.1 * first / (jnp.sqrt(second) + 1e-08)

    input_grad = lax.dot_general(
        masked, weights, (((1,), (1,)), ((), ())), preferred_element_type=jnp.float32
    )
    input_grad = (input_grad * factor).astype(jnp.bfloat16)
    return (input_grad[None], master_out[None], fresh[None], anchor_out[None], momentum_out[None])


def solution(mesh):
    placed = (
        P("replica", "fsdp", None),
        P("replica", "fsdp", None),
        P("replica", "fsdp", None),
        P("replica", "fsdp", None),
        P("replica", "fsdp", None),
        P("replica", None),
        P("replica", "fsdp", None, None),
        P("fsdp", "replica", None),
        P("fsdp", "replica", None),
    )
    return jax.shard_map(
        local,
        mesh=mesh,
        in_specs=placed,
        out_specs=(
            P("replica", "fsdp", None),
            P("replica", "fsdp", None),
            P("fsdp", None, None),
            P("fsdp", "replica", None),
            P("fsdp", "replica", None),
        ),
        check_vma=False,
    )
```

```python
import math

import jax
import jax.numpy as jnp
from jax import lax
from jax.experimental import pallas as pl
from jax.experimental.pallas import tpu as pltpu
from jax.sharding import PartitionSpec as P

QUAD = 4
COLUMN = 4
HALF = jnp.bfloat16
FULL = jnp.float32
SMEM = pl.BlockSpec(memory_space=pltpu.SMEM)
VMEM = pl.BlockSpec(memory_space=pltpu.VMEM)
AC_A2A = False
OUT_A2A = False


def block_of(place, step):
    return place ^ (((step & 1) << 1) | (step >> 1))


def pack_kernel(info, features, cotangent, *packed):
    block = features.shape[1] // (COLUMN * QUAD)
    row = lax.broadcasted_iota(jnp.int32, cotangent.shape, 0)
    masked = jnp.where(row < info[0], cotangent[...], jnp.zeros((), cotangent.dtype))
    for d in range(COLUMN):
        out = packed[0].at[d] if AC_A2A else packed[d]
        y = d if AC_A2A else (info[2] + d) % COLUMN
        for step in range(QUAD):
            source = pl.multiple_of((y * QUAD + block_of(info[1], step)) * block, block)
            out[:, step * block : (step + 1) * block] = features[:, pl.ds(source, block)]
        out[:, QUAD * block :] = masked


def unpack_kernel(info, *refs):
    pieces, result = refs[:-1], refs[-1]
    block = result.shape[1] // (COLUMN * QUAD)
    for d in range(COLUMN):
        piece = pieces[0].at[d] if OUT_A2A else pieces[d]
        y = d if OUT_A2A else (info[2] + d) % COLUMN
        for step in range(QUAD):
            target = pl.multiple_of((y * QUAD + block_of(info[1], step)) * block, block)
            result[:, pl.ds(target, block)] = piece[:, step * block : (step + 1) * block]


def input_kernel(factor, info, own, beside, across, *refs):
    count = 1 if AC_A2A else COLUMN
    cotangents, results = refs[:count], refs[count:]
    tokens, keys = cotangents[0].shape[-2:]
    block = own.shape[0]
    rights = (own[...], beside[...], across[:block], across[block:])
    lefts = []
    for d in range(COLUMN):
        lefts.append(cotangents[0][(info[2] + COLUMN - d) % COLUMN] if AC_A2A else cotangents[d][...])
    left = jnp.concatenate(lefts, axis=0)
    for step, right in enumerate(rights):
        product = lax.dot_general(left, right, (((1,), (1,)), ((), ())), preferred_element_type=FULL)
        product = (product * factor).astype(HALF)
        for d in range(COLUMN):
            part = product[d * tokens : (d + 1) * tokens]
            if OUT_A2A:
                results[0][(info[2] + COLUMN - d) % COLUMN, :, step * block : (step + 1) * block] = part
            else:
                results[d][:, step * block : (step + 1) * block] = part


def weight_kernel(*refs):
    count = 1 if AC_A2A else COLUMN
    packed, (kept, sent) = refs[:count], refs[count:]
    half = kept.shape[0]

    def columns(start, size):
        if AC_A2A:
            part = packed[0][:, :, start : start + size]
            return part.reshape(-1, size)
        return jnp.concatenate([ref[:, start : start + size] for ref in packed], axis=0)

    right = columns(2 * half, kept.shape[1])
    sent[...] = lax.dot_general(
        columns(half, half), right, (((0,), (0,)), ((), ())), preferred_element_type=FULL
    ).astype(HALF)
    kept[...] = lax.dot_general(
        columns(0, half), right, (((0,), (0,)), ((), ())), preferred_element_type=FULL
    )


def whole(shape):
    return pl.BlockSpec(shape, lambda *_: (0,) * len(shape))


def call(kernel, outs, ins, in_specs=None, flops=0, moved=4 << 20, grid=()):
    return pl.pallas_call(
        kernel,
        grid=grid,
        out_shape=outs,
        in_specs=in_specs,
        out_specs=jax.tree.map(lambda s: whole(s.shape), outs),
        compiler_params=pltpu.CompilerParams(vmem_limit_bytes=48 << 20),
        cost_estimate=pl.CostEstimate(flops=flops, bytes_accessed=moved, transcendentals=0),
    )(*ins)


def local(
    activations, cotangent, master, moment_one, moment_two, lengths, pseudo_grad, anchor, momentum
):
    shards = lax.axis_size("fsdp")
    replicas = lax.axis_size("replica")
    fsdp_index = lax.axis_index("fsdp")
    tokens, width = activations.shape[1:]
    keys = cotangent.shape[2]
    share_rows = anchor.shape[1]
    rows = master.shape[1]
    wide = width // COLUMN
    factor = 1.0 / math.sqrt(width)

    columns = [[QUAD * y + j for y in range(COLUMN)] for j in range(QUAD)]
    beside = [(f, f ^ 2) for f in range(shards)]
    across = [(f, f ^ 1) for f in range(shards)]
    up = [[(f, (f + QUAD * d) % shards) for f in range(shards)] for d in range(COLUMN)]
    down = [[(f, (f - QUAD * d) % shards) for f in range(shards)] for d in range(COLUMN)]
    depth = replicas // 2
    outer = depth // QUAD
    nearby = 2 * QUAD
    near = [[depth * h + QUAD * a + b for h in range(2) for b in range(QUAD)] for a in range(outer)]
    far = [[depth * h + QUAD * a + b for a in range(outer)] for h in range(2) for b in range(QUAD)]
    far_place = lax.axis_index("replica") % depth // QUAD

    pieces = pseudo_grad[0, 0].astype(HALF).reshape(2, outer, QUAD, share_rows, keys)
    pieces = pieces.transpose(0, 2, 1, 3, 4).reshape(nearby, outer * share_rows, keys)
    pieces = lax.all_to_all(pieces, "replica", 0, 0, axis_index_groups=near)

    own = master[0].astype(HALF)
    other = lax.ppermute(own, "fsdp", beside)
    both = lax.ppermute(jnp.concatenate([own, other], axis=0), "fsdp", across)

    own_length = lax.dynamic_index_in_dim(lengths[0], fsdp_index, keepdims=False)
    info = jnp.stack([own_length, fsdp_index % QUAD, fsdp_index // QUAD]).astype(jnp.int32)
    one = jax.ShapeDtypeStruct((tokens, wide + keys), HALF)
    packed_shape = jax.ShapeDtypeStruct((COLUMN, *one.shape), HALF) if AC_A2A else one
    packed = list(call(
        pack_kernel,
        [packed_shape] * (1 if AC_A2A else COLUMN),
        (info, activations[0], cotangent[0]),
        [SMEM, VMEM, VMEM],
    ))
    if AC_A2A:
        packed[0], pieces = lax.optimization_barrier((packed[0], pieces))
        packed = [lax.all_to_all(packed[0], "fsdp", 0, 0, axis_index_groups=columns)]
    else:
        packed = [packed[0]] + [lax.ppermute(packed[d], "fsdp", up[d]) for d in range(1, COLUMN)]

    pieces = jnp.sum(pieces.astype(FULL), axis=0).astype(HALF)
    base = anchor[0] - 0.7 * 0.9 * 0.9 * momentum[0]
    high = base.astype(HALF)
    low = (base - high.astype(FULL)).astype(HALF)
    pieces = jnp.concatenate([pieces, high, low], axis=0)
    pieces = jnp.broadcast_to(pieces[None], (outer, *pieces.shape))
    if AC_A2A:
        packed[0], pieces = lax.optimization_barrier((packed[0], pieces))
    pieces = lax.all_to_all(pieces, "replica", 0, 0, axis_index_groups=far)
    delta = jnp.sum(pieces[:, : outer * share_rows].astype(FULL), axis=0) / replicas
    own_delta = lax.dynamic_slice_in_dim(delta, far_place * share_rows, share_rows, 0)
    momentum_out = 0.9 * momentum[0] + own_delta
    anchor_out = anchor[0] - 0.7 * (own_delta + 0.9 * momentum_out)
    bases = pieces[:, outer * share_rows :].astype(FULL)
    bases = (bases[:, :share_rows] + bases[:, share_rows:]).reshape(delta.shape)
    fresh = (bases - 0.7 * 1.9 * delta).astype(HALF)
    fresh = jnp.broadcast_to(fresh[None], (nearby, *fresh.shape))

    cot_spec = (
        pl.BlockSpec((COLUMN, tokens, keys), lambda *_: (0, 0, wide // keys))
        if AC_A2A
        else pl.BlockSpec((tokens, keys), lambda *_: (0, wide // keys))
    )
    out = jax.ShapeDtypeStruct((tokens, wide), HALF)
    out_shape = jax.ShapeDtypeStruct((COLUMN, *out.shape), HALF) if OUT_A2A else out
    products = list(call(
        lambda *refs: input_kernel(factor, *refs),
        [out_shape] * (1 if OUT_A2A else COLUMN),
        (info, own, other, both, *packed),
        [SMEM, whole(own.shape), whole(own.shape), whole(both.shape)] + [cot_spec] * len(packed),
        2 * COLUMN * tokens * wide * keys,
        grid=(1,),
    ))
    if OUT_A2A:
        products[0], fresh = lax.optimization_barrier((products[0], fresh))
        products = [lax.all_to_all(products[0], "fsdp", 0, 0, axis_index_groups=columns)]
        products[0], fresh = lax.optimization_barrier((products[0], fresh))
    else:
        products = [products[0]] + [lax.ppermute(products[d], "fsdp", down[d]) for d in range(1, COLUMN)]
    fresh = lax.all_to_all(fresh, "replica", 0, 0, axis_index_groups=near)
    fresh = fresh.reshape(2, QUAD, outer, share_rows, keys).transpose(0, 2, 1, 3, 4)
    fresh = fresh.reshape(pseudo_grad.shape[2:])

    kept, sent = call(
        weight_kernel,
        [jax.ShapeDtypeStruct((wide // 2, keys), FULL), jax.ShapeDtypeStruct((wide // 2, keys), HALF)],
        packed,
        [VMEM] * len(packed),
        2 * COLUMN * tokens * wide * keys,
    )
    kept = kept + lax.ppermute(sent, "fsdp", across).astype(FULL)
    summed = kept[:rows] + lax.ppermute(kept[rows:].astype(HALF), "fsdp", beside).astype(FULL)

    grad = summed * factor
    first = 0.9 * moment_one[0] + 0.1 * grad
    second = 0.95 * moment_two[0] + 0.05 * grad * grad
    master_out = master[0] * (1.0 - 0.1 * 0.1) - 0.1 * first / (jnp.sqrt(second) + 1e-08)

    (input_grad,) = call(
        unpack_kernel,
        [jax.ShapeDtypeStruct((tokens, width), HALF)],
        (info, *products),
        [SMEM] + [VMEM] * len(products),
        moved=2 << 20,
    )
    return (input_grad[None], master_out[None], fresh[None], anchor_out[None], momentum_out[None])


def solution(mesh):
    placed = (
        P("replica", "fsdp", None),
        P("replica", "fsdp", None),
        P("replica", "fsdp", None),
        P("replica", "fsdp", None),
        P("replica", "fsdp", None),
        P("replica", None),
        P("replica", "fsdp", None, None),
        P("fsdp", "replica", None),
        P("fsdp", "replica", None),
    )
    return jax.shard_map(
        local,
        mesh=mesh,
        in_specs=placed,
        out_specs=(
            P("replica", "fsdp", None),
            P("replica", "fsdp", None),
            P("fsdp", None, None),
            P("fsdp", "replica", None),
            P("fsdp", "replica", None),
        ),
        check_vma=False,
    )
```

```python
import math

import jax
import jax.numpy as jnp
from jax import lax
from jax.experimental import pallas as pl
from jax.experimental.pallas import tpu as pltpu
from jax.sharding import PartitionSpec as P

QUAD = 4
COLUMN = 4
SIDES = 2
NEAR = SIDES * QUAD
NEAR_ORDER = ((0, 1), (0, 2), (0, 0), (0, 3), (1, 1), (1, 2), (1, 0), (1, 3))
FAR_ORDER = (2, 3, 1, 0)
HALF = jnp.bfloat16
FULL = jnp.float32
SMEM = pl.BlockSpec(memory_space=pltpu.SMEM)
VMEM = pl.BlockSpec(memory_space=pltpu.VMEM)
ANY = pl.BlockSpec(memory_space=pl.ANY)


def block_of(place, step):
    return place ^ (((step & 1) << 1) | (step >> 1))


def split_kernel(whole, pieces):
    share = pieces.shape[1] // COLUMN
    far = pieces.shape[1] // share
    for i, (h, b) in enumerate(NEAR_ORDER):
        starts = [((h * far + a) * QUAD + b) * share for a in range(far)]
        rows = [whole[start : start + share] for start in starts]
        pieces[i] = jnp.concatenate(rows, axis=0).astype(HALF)


def join_kernel(pieces, whole):
    share = pieces.shape[1] // COLUMN
    far = pieces.shape[1] // share
    parts = {key: pieces[i].astype(FULL) for i, key in enumerate(NEAR_ORDER)}
    for h in range(SIDES):
        for a in range(far):
            rows = [parts[h, b][a * share : (a + 1) * share] for b in range(QUAD)]
            start = (h * far + a) * QUAD * share
            whole[start : start + QUAD * share] = jnp.concatenate(rows, axis=0).astype(HALF)


def pack_kernel(lengths, features, cotangent, after, *packed):
    me = lax.axis_index("fsdp")
    place, y = me % QUAD, me // QUAD
    block = features.shape[1] // (COLUMN * QUAD)
    row = lax.broadcasted_iota(jnp.int32, cotangent.shape, 0)
    masked = jnp.where(row < lengths[0, me], cotangent[...], jnp.zeros((), cotangent.dtype))
    for d in range(COLUMN):
        target = (y + d) % COLUMN
        for step in range(QUAD):
            source = pl.multiple_of((target * QUAD + block_of(place, step)) * block, block)
            packed[d][:, step * block : (step + 1) * block] = features[:, pl.ds(source, block)]
        packed[d][:, QUAD * block :] = masked


def sum_kernel(pieces, anchor, momentum, after, sums):
    total = pieces[0].astype(FULL)
    for i in range(1, NEAR):
        total += pieces[i].astype(FULL)
    base = anchor[...] - 0.7 * 0.9 * 0.9 * momentum[...]
    high = base.astype(HALF).astype(FULL)
    value = jnp.concatenate([total, high, base - high], axis=0).astype(HALF)
    for i in range(sums.shape[0]):
        sums[i] = value


def update_kernel(sums, anchor, momentum, anchor_out, momentum_out, fresh, delta):
    share = anchor.shape[0]
    far = sums.shape[0]
    near_rows = far * share
    parts = [sums[i].astype(FULL) for i in range(far)]
    total = parts[0][:near_rows]
    for part in parts[1:]:
        total += part[:near_rows]
    total = total / (NEAR * far)
    delta[...] = total
    place = lax.axis_index("replica") // QUAD % far
    own = delta[pl.ds(pl.multiple_of(place * share, share), share), :]
    moved = 0.9 * momentum[...] + own
    momentum_out[...] = moved
    anchor_out[...] = anchor[...] - 0.7 * (own + 0.9 * moved)
    parts = [parts[FAR_ORDER.index(a)][near_rows:] for a in range(far)]
    bases = [part[:share] + part[share:] for part in parts]
    value = (jnp.concatenate(bases, axis=0) - 0.7 * 1.9 * total).astype(HALF)
    for i in range(NEAR):
        fresh[i] = value


def input_kernel(factor, after, own, beside, across, *refs):
    cotangents, results = refs[:COLUMN], refs[COLUMN:]
    tokens = cotangents[0].shape[0]
    block = own.shape[0]
    left = jnp.concatenate([ref[...] for ref in cotangents], axis=0)
    for step, right in enumerate((own[...], beside[...], across[:block], across[block:])):
        product = lax.dot_general(left, right, (((1,), (1,)), ((), ())), preferred_element_type=FULL)
        product = (product * factor).astype(HALF)
        for d in range(COLUMN):
            results[d][:, step * block : (step + 1) * block] = product[d * tokens : (d + 1) * tokens]


def weight_kernel(*refs):
    packed, (after, own, passed, sent) = refs[:COLUMN], refs[COLUMN:]
    rows, keys = own.shape

    def columns(start, size):
        return jnp.concatenate([ref[:, start : start + size] for ref in packed], axis=0)

    def term(start, size):
        return lax.dot_general(
            columns(start, size), right, (((0,), (0,)), ((), ())), preferred_element_type=FULL
        )

    right = columns(QUAD * rows, keys)
    sent[...] = term(2 * rows, 2 * rows).astype(HALF)
    own[...] = term(0, rows)
    passed[...] = term(rows, rows)


def unpack_kernel(*refs):
    pieces, result, done = refs[:COLUMN], refs[COLUMN], refs[COLUMN + 1]
    me = lax.axis_index("fsdp")
    place, y = me % QUAD, me // QUAD
    block = result.shape[1] // (COLUMN * QUAD)
    copies = []
    for d in range(COLUMN):
        for step in range(QUAD):
            target = ((y + d) % COLUMN * QUAD + block_of(place, step)) * block
            copies.append(
                pltpu.make_async_copy(
                    pieces[d].at[:, pl.ds(step * block, block)],
                    result.at[:, pl.ds(pl.multiple_of(target, block), block)],
                    done.at[d * QUAD + step],
                )
            )
    for copy in copies:
        copy.start()
    for copy in copies:
        copy.wait()


def whole(shape):
    return pl.BlockSpec(shape, lambda *_: (0,) * len(shape))


def call(kernel, outs, ins, in_specs=None, out_specs=None, flops=0, moved=1 << 20, scratch=(), grid=()):
    outs = [jax.ShapeDtypeStruct(shape, dtype) for shape, dtype in outs]
    return pl.pallas_call(
        kernel,
        grid=grid,
        out_shape=outs,
        in_specs=in_specs or [VMEM] * len(ins),
        out_specs=out_specs or [whole(out.shape) for out in outs],
        scratch_shapes=scratch,
        compiler_params=pltpu.CompilerParams(vmem_limit_bytes=48 << 20),
        cost_estimate=pl.CostEstimate(flops=flops, bytes_accessed=moved, transcendentals=0),
    )(*ins)


def local(
    activations, cotangent, master, moment_one, moment_two, lengths, pseudo_grad, anchor, momentum
):
    shards = lax.axis_size("fsdp")
    replicas = lax.axis_size("replica")
    tokens, width = activations.shape[1:]
    keys = cotangent.shape[2]
    share = anchor.shape[1]
    rows = master.shape[1]
    wide = width // COLUMN
    factor = 1.0 / math.sqrt(width)
    flops = 2 * COLUMN * tokens * wide * keys

    beside = [(f, f ^ 2) for f in range(shards)]
    across = [(f, f ^ 1) for f in range(shards)]
    up = [[(f, (f + QUAD * d) % shards) for f in range(shards)] for d in range(COLUMN)]
    down = [[(f, (f - QUAD * d) % shards) for f in range(shards)] for d in range(COLUMN)]
    depth = replicas // SIDES
    outer = depth // QUAD
    near = [[depth * h + QUAD * a + b for h, b in NEAR_ORDER] for a in range(outer)]
    far = [[depth * h + QUAD * a + b for a in FAR_ORDER] for h in range(SIDES) for b in range(QUAD)]

    (pieces,) = call(split_kernel, [((NEAR, outer * share, keys), HALF)], (pseudo_grad[0, 0],))
    near_pieces = lax.all_to_all(pieces, "replica", 0, 0, axis_index_groups=near)

    packed = call(
        pack_kernel,
        [((tokens, wide + keys), HALF)] * COLUMN,
        (lengths, activations[0], cotangent[0], pieces),
        [SMEM, VMEM, VMEM, ANY],
        moved=3 << 20,
    )
    packed = [packed[0]] + [lax.ppermute(packed[d], "fsdp", up[d]) for d in (1, 2, 3)]

    raw = lax.optimization_barrier((master[0], packed[0]))[0]
    own = raw.astype(HALF)
    other = lax.ppermute(own, "fsdp", beside)

    (sums,) = call(
        sum_kernel,
        [((outer, (outer + 2) * share, keys), HALF)],
        (near_pieces, anchor[0], momentum[0], packed[0]),
        [VMEM, VMEM, VMEM, ANY],
    )
    other = lax.optimization_barrier((other, sums, packed[1], packed[2], packed[3]))[0]
    both = lax.ppermute(jnp.concatenate([own, other], axis=0), "fsdp", across)
    sums = lax.all_to_all(sums, "replica", 0, 0, axis_index_groups=far)
    anchor_out, momentum_out, fresh = call(
        update_kernel,
        [((share, keys), FULL), ((share, keys), FULL), ((NEAR, outer * share, keys), HALF)],
        (sums, anchor[0], momentum[0]),
        scratch=[pltpu.VMEM((outer * share, keys), FULL)],
    )
    spread = lax.all_to_all(fresh, "replica", 0, 0, axis_index_groups=near)
    (spread,) = call(join_kernel, [(pseudo_grad.shape[2:], HALF)], (spread,))

    cot_spec = pl.BlockSpec((tokens, keys), lambda *_: (0, wide // keys))
    products = call(
        lambda *refs: input_kernel(factor, *refs),
        [((tokens, wide), HALF)] * COLUMN,
        (fresh, own, other, both, *packed),
        [ANY, whole(own.shape), whole(own.shape), whole(both.shape)] + [cot_spec] * COLUMN,
        flops=flops,
        moved=3 << 20,
        grid=(1,),
    )
    back = [products[0]] + [lax.ppermute(products[d], "fsdp", down[d]) for d in (1, 2, 3)]

    grad_own, grad_passed, sent = call(
        weight_kernel,
        [((rows, keys), FULL), ((rows, keys), FULL), ((2 * rows, keys), HALF)],
        (*packed, products[0]),
        [VMEM] * COLUMN + [ANY],
        flops=flops,
        moved=5 << 20,
    )
    crossed = lax.ppermute(sent, "fsdp", across).astype(FULL)
    passed = lax.ppermute((grad_passed + crossed[rows:]).astype(HALF), "fsdp", beside)
    summed = grad_own + crossed[:rows] + passed.astype(FULL)

    grad = summed * factor
    first = 0.9 * moment_one[0] + 0.1 * grad
    second = 0.95 * moment_two[0] + 0.05 * grad * grad
    master_out = master[0] * (1.0 - 0.1 * 0.1) - 0.1 * first / (jnp.sqrt(second) + 1e-08)

    (input_grad,) = call(
        unpack_kernel,
        [((tokens, width), HALF)],
        back,
        [ANY] * COLUMN,
        [ANY],
        scratch=[pltpu.SemaphoreType.DMA((COLUMN * QUAD,))],
        moved=2 << 20,
    )
    return (
        input_grad[None], master_out[None], spread[None], anchor_out[None], momentum_out[None]
    )


def solution(mesh):
    placed = (
        P("replica", "fsdp", None),
        P("replica", "fsdp", None),
        P("replica", "fsdp", None),
        P("replica", "fsdp", None),
        P("replica", "fsdp", None),
        P("replica", None),
        P("replica", "fsdp", None, None),
        P("fsdp", "replica", None),
        P("fsdp", "replica", None),
    )
    return jax.shard_map(
        local,
        mesh=mesh,
        in_specs=placed,
        out_specs=(
            P("replica", "fsdp", None),
            P("replica", "fsdp", None),
            P("fsdp", None, None),
            P("fsdp", "replica", None),
            P("fsdp", "replica", None),
        ),
        check_vma=False,
    )
```

```python
import math

import jax
import jax.numpy as jnp
from jax import lax
from jax.experimental import pallas as pl
from jax.experimental.pallas import tpu as pltpu
from jax.sharding import PartitionSpec as P

QUAD = 4
COLUMN = 4
SIDES = 2
NEAR = SIDES * QUAD
NEAR_ORDER = ((1, 1), (1, 2), (0, 1), (0, 2), (1, 0), (1, 3), (0, 0), (0, 3))
FAR_ORDER = (2, 3, 1, 0)
HALF = jnp.bfloat16
FULL = jnp.float32
SMEM = pl.BlockSpec(memory_space=pltpu.SMEM)
VMEM = pl.BlockSpec(memory_space=pltpu.VMEM)
ANY = pl.BlockSpec(memory_space=pl.ANY)


def block_of(place, step):
    return place ^ (((step & 1) << 1) | (step >> 1))


def split_kernel(whole, pieces):
    share = pieces.shape[1] // COLUMN
    far = pieces.shape[1] // share
    for i, (h, b) in enumerate(NEAR_ORDER):
        starts = [((h * far + a) * QUAD + b) * share for a in range(far)]
        rows = [whole[start : start + share] for start in starts]
        pieces[i] = jnp.concatenate(rows, axis=0).astype(HALF)


def join_kernel(pieces, whole):
    share = pieces.shape[1] // COLUMN
    far = pieces.shape[1] // share
    parts = {key: pieces[i].astype(FULL) for i, key in enumerate(NEAR_ORDER)}
    for h in range(SIDES):
        for a in range(far):
            rows = [parts[h, b][a * share : (a + 1) * share] for b in range(QUAD)]
            start = (h * far + a) * QUAD * share
            whole[start : start + QUAD * share] = jnp.concatenate(rows, axis=0).astype(HALF)


def pack_kernel(lengths, features, cotangent, after, *packed):
    me = lax.axis_index("fsdp")
    place, y = me % QUAD, me // QUAD
    block = features.shape[1] // (COLUMN * QUAD)
    row = lax.broadcasted_iota(jnp.int32, cotangent.shape, 0)
    masked = jnp.where(row < lengths[0, me], cotangent[...], jnp.zeros((), cotangent.dtype))
    for d in range(COLUMN):
        target = (y + d) % COLUMN
        for step in range(QUAD):
            source = pl.multiple_of((target * QUAD + block_of(place, step)) * block, block)
            packed[d][:, step * block : (step + 1) * block] = features[:, pl.ds(source, block)]
        packed[d][:, QUAD * block :] = masked


def sum_kernel(pieces, anchor, momentum, after, later, sums):
    total = pieces[0].astype(FULL)
    for i in range(1, NEAR):
        total += pieces[i].astype(FULL)
    base = anchor[...] - 0.7 * 0.9 * 0.9 * momentum[...]
    high = base.astype(HALF).astype(FULL)
    value = jnp.concatenate([total, high, base - high], axis=0).astype(HALF)
    for i in range(sums.shape[0]):
        sums[i] = value


def update_kernel(sums, anchor, momentum, anchor_out, momentum_out, fresh, delta):
    share = anchor.shape[0]
    far = sums.shape[0]
    near_rows = far * share
    parts = [sums[i].astype(FULL) for i in range(far)]
    total = parts[0][:near_rows]
    for part in parts[1:]:
        total += part[:near_rows]
    total = total / (NEAR * far)
    delta[...] = total
    place = lax.axis_index("replica") // QUAD % far
    own = delta[pl.ds(pl.multiple_of(place * share, share), share), :]
    moved = 0.9 * momentum[...] + own
    momentum_out[...] = moved
    anchor_out[...] = anchor[...] - 0.7 * (own + 0.9 * moved)
    parts = [parts[FAR_ORDER.index(a)][near_rows:] for a in range(far)]
    bases = [part[:share] + part[share:] for part in parts]
    value = (jnp.concatenate(bases, axis=0) - 0.7 * 1.9 * total).astype(HALF)
    for i in range(NEAR):
        fresh[i] = value


def input_kernel(factor, after, own, beside, across, *refs):
    cotangents, results = refs[:COLUMN], refs[COLUMN]
    y = lax.axis_index("fsdp") // QUAD
    tokens = cotangents[0].shape[0]
    block = own.shape[0]
    left = jnp.concatenate([ref[...] for ref in cotangents], axis=0)
    for step, right in enumerate((own[...], beside[...], across[:block], across[block:])):
        product = lax.dot_general(left, right, (((1,), (1,)), ((), ())), preferred_element_type=FULL)
        product = (product * factor).astype(HALF)
        for d in range(COLUMN):
            part = product[d * tokens : (d + 1) * tokens]
            results[(y + COLUMN - d) % COLUMN, :, step * block : (step + 1) * block] = part


def weight_kernel(*refs):
    packed, (after, own, passed, sent) = refs[:COLUMN], refs[COLUMN:]
    rows, keys = own.shape

    def columns(start, size):
        return jnp.concatenate([ref[:, start : start + size] for ref in packed], axis=0)

    def term(start, size):
        return lax.dot_general(
            columns(start, size), right, (((0,), (0,)), ((), ())), preferred_element_type=FULL
        )

    right = columns(QUAD * rows, keys)
    sent[...] = term(2 * rows, 2 * rows).astype(HALF)
    own[...] = term(0, rows)
    passed[...] = term(rows, rows)


def unpack_kernel(*refs):
    pieces, result, done = refs
    place = lax.axis_index("fsdp") % QUAD
    block = result.shape[1] // (COLUMN * QUAD)
    copies = []
    for d in range(COLUMN):
        for step in range(QUAD):
            target = (d * QUAD + block_of(place, step)) * block
            copies.append(
                pltpu.make_async_copy(
                    pieces.at[d, :, pl.ds(step * block, block)],
                    result.at[:, pl.ds(pl.multiple_of(target, block), block)],
                    done.at[d * QUAD + step],
                )
            )
    for copy in copies:
        copy.start()
    for copy in copies:
        copy.wait()


def whole(shape):
    return pl.BlockSpec(shape, lambda *_: (0,) * len(shape))


def call(kernel, outs, ins, in_specs=None, out_specs=None, flops=0, moved=1 << 20, scratch=(), grid=()):
    outs = [jax.ShapeDtypeStruct(shape, dtype) for shape, dtype in outs]
    return pl.pallas_call(
        kernel,
        grid=grid,
        out_shape=outs,
        in_specs=in_specs or [VMEM] * len(ins),
        out_specs=out_specs or [whole(out.shape) for out in outs],
        scratch_shapes=scratch,
        compiler_params=pltpu.CompilerParams(vmem_limit_bytes=48 << 20),
        cost_estimate=pl.CostEstimate(flops=flops, bytes_accessed=moved, transcendentals=0),
    )(*ins)


def local(
    activations, cotangent, master, moment_one, moment_two, lengths, pseudo_grad, anchor, momentum
):
    shards = lax.axis_size("fsdp")
    replicas = lax.axis_size("replica")
    tokens, width = activations.shape[1:]
    keys = cotangent.shape[2]
    share = anchor.shape[1]
    rows = master.shape[1]
    wide = width // COLUMN
    factor = 1.0 / math.sqrt(width)
    flops = 2 * COLUMN * tokens * wide * keys

    beside = [(f, f ^ 2) for f in range(shards)]
    across = [(f, f ^ 1) for f in range(shards)]
    up = [[(f, (f + QUAD * d) % shards) for f in range(shards)] for d in range(COLUMN)]
    columns = [[QUAD * y + j for y in range(COLUMN)] for j in range(QUAD)]
    depth = replicas // SIDES
    outer = depth // QUAD
    near = [[depth * h + QUAD * a + b for h, b in NEAR_ORDER] for a in range(outer)]
    far = [[depth * h + QUAD * a + b for a in FAR_ORDER] for h in range(SIDES) for b in range(QUAD)]

    (pieces,) = call(split_kernel, [((NEAR, outer * share, keys), HALF)], (pseudo_grad[0, 0],))
    near_pieces = lax.all_to_all(pieces, "replica", 0, 0, axis_index_groups=near)

    packed = call(
        pack_kernel,
        [((tokens, wide + keys), HALF)] * COLUMN,
        (lengths, activations[0], cotangent[0], pieces),
        [SMEM, VMEM, VMEM, ANY],
        moved=3 << 20,
    )
    packed = [packed[0]] + [lax.ppermute(packed[d], "fsdp", up[d]) for d in (1, 2, 3)]

    raw = lax.optimization_barrier((master[0], packed[0]))[0]
    own = raw.astype(HALF)
    other = lax.ppermute(own, "fsdp", beside)

    (sums,) = call(
        sum_kernel,
        [((outer, (outer + 2) * share, keys), HALF)],
        (near_pieces, anchor[0], momentum[0], packed[0], other),
        [VMEM, VMEM, VMEM, ANY, ANY],
    )
    other = lax.optimization_barrier((other, sums, packed[2], packed[3]))[0]
    both = lax.ppermute(jnp.concatenate([own, other], axis=0), "fsdp", across)
    sums = lax.all_to_all(sums, "replica", 0, 0, axis_index_groups=far)
    anchor_out, momentum_out, fresh = call(
        update_kernel,
        [((share, keys), FULL), ((share, keys), FULL), ((NEAR, outer * share, keys), HALF)],
        (sums, anchor[0], momentum[0]),
        scratch=[pltpu.VMEM((outer * share, keys), FULL)],
    )

    cot_spec = pl.BlockSpec((tokens, keys), lambda *_: (0, wide // keys))
    (products,) = call(
        lambda *refs: input_kernel(factor, *refs),
        [((COLUMN, tokens, wide), HALF)],
        (fresh, own, other, both, *packed),
        [ANY, whole(own.shape), whole(own.shape), whole(both.shape)] + [cot_spec] * COLUMN,
        flops=flops,
        moved=3 << 20,
        grid=(1,),
    )
    spread = lax.all_to_all(fresh, "replica", 0, 0, axis_index_groups=near)
    outgoing, spread = lax.optimization_barrier((products, spread))
    back = lax.all_to_all(outgoing, "fsdp", 0, 0, axis_index_groups=columns)
    (spread,) = call(join_kernel, [(pseudo_grad.shape[2:], HALF)], (spread,))

    grad_own, grad_passed, sent = call(
        weight_kernel,
        [((rows, keys), FULL), ((rows, keys), FULL), ((2 * rows, keys), HALF)],
        (*packed, products),
        [VMEM] * COLUMN + [ANY],
        flops=flops,
        moved=5 << 20,
    )
    crossed = lax.ppermute(sent, "fsdp", across)
    passed = lax.ppermute((grad_passed + crossed[rows:].astype(FULL)).astype(HALF), "fsdp", beside)
    summed = grad_own + crossed[:rows].astype(FULL) + passed.astype(FULL)

    grad = summed * factor
    first = 0.9 * moment_one[0] + 0.1 * grad
    second = 0.95 * moment_two[0] + 0.05 * grad * grad
    master_out = master[0] * (1.0 - 0.1 * 0.1) - 0.1 * first / (jnp.sqrt(second) + 1e-08)

    (input_grad,) = call(
        unpack_kernel,
        [((tokens, width), HALF)],
        (back,),
        [ANY],
        [ANY],
        scratch=[pltpu.SemaphoreType.DMA((COLUMN * QUAD,))],
        moved=2 << 20,
    )
    return (
        input_grad[None], master_out[None], spread[None], anchor_out[None], momentum_out[None]
    )


def solution(mesh):
    placed = (
        P("replica", "fsdp", None),
        P("replica", "fsdp", None),
        P("replica", "fsdp", None),
        P("replica", "fsdp", None),
        P("replica", "fsdp", None),
        P("replica", None),
        P("replica", "fsdp", None, None),
        P("fsdp", "replica", None),
        P("fsdp", "replica", None),
    )
    return jax.shard_map(
        local,
        mesh=mesh,
        in_specs=placed,
        out_specs=(
            P("replica", "fsdp", None),
            P("replica", "fsdp", None),
            P("fsdp", None, None),
            P("fsdp", "replica", None),
            P("fsdp", "replica", None),
        ),
        check_vma=False,
    )
```

```python
import math

import jax
import jax.numpy as jnp
from jax import lax
from jax.experimental import pallas as pl
from jax.experimental.pallas import tpu as pltpu
from jax.sharding import PartitionSpec as P

QUAD = 4
COLUMN = 4
SIDES = 2
NEAR = SIDES * QUAD
NEAR_ORDER = ((1, 1), (1, 2), (0, 1), (0, 2), (1, 0), (1, 3), (0, 0), (0, 3))
FAR_ORDER = (2, 3, 1, 0)
LEAD = 2
HALF = jnp.bfloat16
FULL = jnp.float32
VMEM = pl.BlockSpec(memory_space=pltpu.VMEM)
ANY = pl.BlockSpec(memory_space=pl.ANY)


def block_of(place, step):
    return place ^ (((step & 1) << 1) | (step >> 1))


def split_kernel(whole, pieces):
    share = pieces.shape[1] // COLUMN
    far = pieces.shape[1] // share
    for i, (h, b) in enumerate(NEAR_ORDER):
        starts = [((h * far + a) * QUAD + b) * share for a in range(far)]
        rows = [whole[start : start + share] for start in starts]
        pieces[i] = jnp.concatenate(rows, axis=0).astype(HALF)


def join_kernel(pieces, whole):
    share = pieces.shape[1] // COLUMN
    far = pieces.shape[1] // share
    parts = {key: pieces[i].astype(FULL) for i, key in enumerate(NEAR_ORDER)}
    for h in range(SIDES):
        for a in range(far):
            rows = [parts[h, b][a * share : (a + 1) * share] for b in range(QUAD)]
            start = (h * far + a) * QUAD * share
            whole[start : start + QUAD * share] = jnp.concatenate(rows, axis=0).astype(HALF)


def pack_kernel(lengths, features, cotangent, after, *packed):
    me = lax.axis_index("fsdp")
    place, y = me % QUAD, me // QUAD
    block = features.shape[1] // (COLUMN * QUAD)
    mine = lax.broadcasted_iota(jnp.int32, lengths.shape, 1) == me
    own = jnp.sum(jnp.where(mine, lengths[...].astype(FULL), 0.0), axis=1, keepdims=True)
    row = lax.broadcasted_iota(jnp.int32, cotangent.shape, 0).astype(FULL)
    masked = jnp.where(row < own, cotangent[...], jnp.zeros((), cotangent.dtype))
    for d in range(COLUMN):
        target = (y + d) % COLUMN
        for step in range(QUAD):
            source = pl.multiple_of((target * QUAD + block_of(place, step)) * block, block)
            packed[d][:, step * block : (step + 1) * block] = features[:, pl.ds(source, block)]
        packed[d][:, QUAD * block :] = masked


def sum_kernel(pieces, anchor, momentum, after, later, sums):
    total = pieces[0].astype(FULL)
    for i in range(1, NEAR):
        total += pieces[i].astype(FULL)
    base = anchor[...] - 0.7 * 0.9 * 0.9 * momentum[...]
    high = base.astype(HALF).astype(FULL)
    value = jnp.concatenate([total, high, base - high], axis=0).astype(HALF)
    for i in range(sums.shape[0]):
        sums[i] = value


def update_kernel(sums, anchor, momentum, anchor_out, momentum_out, fresh, delta):
    share = anchor.shape[0]
    far = sums.shape[0]
    near_rows = far * share
    parts = [sums[i].astype(FULL) for i in range(far)]
    total = parts[0][:near_rows]
    for part in parts[1:]:
        total += part[:near_rows]
    total = total / (NEAR * far)
    delta[...] = total
    place = lax.axis_index("replica") // QUAD % far
    own = delta[pl.ds(pl.multiple_of(place * share, share), share), :]
    moved = 0.9 * momentum[...] + own
    momentum_out[...] = moved
    anchor_out[...] = anchor[...] - 0.7 * (own + 0.9 * moved)
    parts = [parts[FAR_ORDER.index(a)][near_rows:] for a in range(far)]
    bases = [part[:share] + part[share:] for part in parts]
    value = (jnp.concatenate(bases, axis=0) - 0.7 * 1.9 * total).astype(HALF)
    for i in range(NEAR):
        fresh[i] = value


def input_kernel(factor, after, own, beside, across, *refs):
    cotangents, results = refs[:COLUMN], refs[COLUMN]
    y = lax.axis_index("fsdp") // QUAD
    tokens = cotangents[0].shape[0]
    block = own.shape[0]
    left = jnp.concatenate([ref[...] for ref in cotangents], axis=0)
    for step, right in enumerate((own[...], beside[...], across[:block], across[block:])):
        product = lax.dot_general(left, right, (((1,), (1,)), ((), ())), preferred_element_type=FULL)
        product = (product * factor).astype(HALF)
        for d in range(COLUMN):
            part = product[d * tokens : (d + 1) * tokens]
            results[(y + 2 * COLUMN - d - LEAD) % COLUMN, :, step * block : (step + 1) * block] = part


def weight_kernel(*refs):
    packed, (after, own, passed, sent) = refs[:COLUMN], refs[COLUMN:]
    rows, keys = own.shape

    def columns(start, size):
        return jnp.concatenate([ref[:, start : start + size] for ref in packed], axis=0)

    def term(start, size):
        return lax.dot_general(
            columns(start, size), right, (((0,), (0,)), ((), ())), preferred_element_type=FULL
        )

    right = columns(QUAD * rows, keys)
    sent[...] = term(2 * rows, 2 * rows).astype(HALF)
    own[...] = term(0, rows)
    passed[...] = term(rows, rows)


def unpack_kernel(*refs):
    pieces, result, done = refs
    place = lax.axis_index("fsdp") % QUAD
    block = result.shape[1] // (COLUMN * QUAD)
    copies = []
    for d in range(COLUMN):
        for step in range(QUAD):
            target = ((d + LEAD) % COLUMN * QUAD + block_of(place, step)) * block
            copies.append(
                pltpu.make_async_copy(
                    pieces.at[d, :, pl.ds(step * block, block)],
                    result.at[:, pl.ds(pl.multiple_of(target, block), block)],
                    done.at[d * QUAD + step],
                )
            )
    for copy in copies:
        copy.start()
    for copy in copies:
        copy.wait()


def whole(shape):
    return pl.BlockSpec(shape, lambda *_: (0,) * len(shape))


def call(kernel, outs, ins, in_specs=None, out_specs=None, flops=0, moved=1 << 20, scratch=(), grid=()):
    outs = [jax.ShapeDtypeStruct(shape, dtype) for shape, dtype in outs]
    return pl.pallas_call(
        kernel,
        grid=grid,
        out_shape=outs,
        in_specs=in_specs or [VMEM] * len(ins),
        out_specs=out_specs or [whole(out.shape) for out in outs],
        scratch_shapes=scratch,
        compiler_params=pltpu.CompilerParams(vmem_limit_bytes=48 << 20),
        cost_estimate=pl.CostEstimate(flops=flops, bytes_accessed=moved, transcendentals=0),
    )(*ins)


def local(
    activations, cotangent, master, moment_one, moment_two, lengths, pseudo_grad, anchor, momentum
):
    shards = lax.axis_size("fsdp")
    replicas = lax.axis_size("replica")
    tokens, width = activations.shape[1:]
    keys = cotangent.shape[2]
    share = anchor.shape[1]
    rows = master.shape[1]
    wide = width // COLUMN
    factor = 1.0 / math.sqrt(width)
    flops = 2 * COLUMN * tokens * wide * keys

    beside = [(f, f ^ 2) for f in range(shards)]
    across = [(f, f ^ 1) for f in range(shards)]
    up = [[(f, (f + QUAD * d) % shards) for f in range(shards)] for d in range(COLUMN)]
    columns = [[QUAD * ((y + LEAD) % COLUMN) + j for y in range(COLUMN)] for j in range(QUAD)]
    depth = replicas // SIDES
    outer = depth // QUAD
    near = [[depth * h + QUAD * a + b for h, b in NEAR_ORDER] for a in range(outer)]
    far = [[depth * h + QUAD * a + b for a in FAR_ORDER] for h in range(SIDES) for b in range(QUAD)]

    (pieces,) = call(split_kernel, [((NEAR, outer * share, keys), HALF)], (pseudo_grad[0, 0],))
    near_pieces = lax.all_to_all(pieces, "replica", 0, 0, axis_index_groups=near)

    packed = call(
        pack_kernel,
        [((tokens, wide + keys), HALF)] * COLUMN,
        (lengths, activations[0], cotangent[0], pieces),
        [VMEM, VMEM, VMEM, ANY],
        moved=3 << 20,
    )
    packed = [packed[0]] + [lax.ppermute(packed[d], "fsdp", up[d]) for d in (1, 2, 3)]

    raw = lax.optimization_barrier((master[0], packed[0]))[0]
    own = raw.astype(HALF)
    other = lax.ppermute(own, "fsdp", beside)

    (sums,) = call(
        sum_kernel,
        [((outer, (outer + 2) * share, keys), HALF)],
        (near_pieces, anchor[0], momentum[0], packed[0], other),
        [VMEM, VMEM, VMEM, ANY, ANY],
    )
    other = lax.optimization_barrier((other, sums, packed[2], packed[3]))[0]
    both = lax.ppermute(jnp.concatenate([own, other], axis=0), "fsdp", across)
    sums = lax.all_to_all(sums, "replica", 0, 0, axis_index_groups=far)
    anchor_out, momentum_out, fresh = call(
        update_kernel,
        [((share, keys), FULL), ((share, keys), FULL), ((NEAR, outer * share, keys), HALF)],
        (sums, anchor[0], momentum[0]),
        scratch=[pltpu.VMEM((outer * share, keys), FULL)],
    )

    cot_spec = pl.BlockSpec((tokens, keys), lambda *_: (0, wide // keys))
    (products,) = call(
        lambda *refs: input_kernel(factor, *refs),
        [((COLUMN, tokens, wide), HALF)],
        (fresh, own, other, both, *packed),
        [ANY, whole(own.shape), whole(own.shape), whole(both.shape)] + [cot_spec] * COLUMN,
        flops=flops,
        moved=3 << 20,
        grid=(1,),
    )
    spread = lax.all_to_all(fresh, "replica", 0, 0, axis_index_groups=near)
    outgoing, spread = lax.optimization_barrier((products, spread))
    back = lax.all_to_all(outgoing, "fsdp", 0, 0, axis_index_groups=columns)
    (spread,) = call(join_kernel, [(pseudo_grad.shape[2:], HALF)], (spread,))

    grad_own, grad_passed, sent = call(
        weight_kernel,
        [((rows, keys), FULL), ((rows, keys), FULL), ((2 * rows, keys), HALF)],
        (*packed, products),
        [VMEM] * COLUMN + [ANY],
        flops=flops,
        moved=5 << 20,
    )
    crossed = lax.ppermute(sent, "fsdp", across)
    passed = lax.ppermute((grad_passed + crossed[rows:].astype(FULL)).astype(HALF), "fsdp", beside)
    summed = lax.optimization_barrier(grad_own + crossed[:rows].astype(FULL))
    passed = lax.optimization_barrier((passed, spread))[0]
    summed = summed + passed.astype(FULL)

    grad = summed * factor
    first = 0.9 * moment_one[0] + 0.1 * grad
    second = 0.95 * moment_two[0] + 0.05 * grad * grad
    master_out = master[0] * (1.0 - 0.1 * 0.1) - 0.1 * first / (jnp.sqrt(second) + 1e-08)

    (input_grad,) = call(
        unpack_kernel,
        [((tokens, width), HALF)],
        (back,),
        [ANY],
        [ANY],
        scratch=[pltpu.SemaphoreType.DMA((COLUMN * QUAD,))],
        moved=2 << 20,
    )
    return (
        input_grad[None], master_out[None], spread[None], anchor_out[None], momentum_out[None]
    )


def solution(mesh):
    placed = (
        P("replica", "fsdp", None),
        P("replica", "fsdp", None),
        P("replica", "fsdp", None),
        P("replica", "fsdp", None),
        P("replica", "fsdp", None),
        P("replica", None),
        P("replica", "fsdp", None, None),
        P("fsdp", "replica", None),
        P("fsdp", "replica", None),
    )
    return jax.shard_map(
        local,
        mesh=mesh,
        in_specs=placed,
        out_specs=(
            P("replica", "fsdp", None),
            P("replica", "fsdp", None),
            P("fsdp", None, None),
            P("fsdp", "replica", None),
            P("fsdp", "replica", None),
        ),
        check_vma=False,
    )
```

```python
import math

import jax
import jax.numpy as jnp
from jax import lax
from jax.experimental import pallas as pl
from jax.experimental.pallas import tpu as pltpu
from jax.sharding import PartitionSpec as P

QUAD = 4
COLUMN = 4
SIDES = 2
NEAR = SIDES * QUAD
NEAR_ORDER = ((1, 2), (1, 1), (0, 2), (0, 1), (1, 3), (1, 0), (0, 3), (0, 0))
FAR_ORDER = (2, 3, 1, 0)
LEAD = 2
HALF = jnp.bfloat16
FULL = jnp.float32
VMEM = pl.BlockSpec(memory_space=pltpu.VMEM)
ANY = pl.BlockSpec(memory_space=pl.ANY)


def block_of(place, step):
    return place ^ (((step & 1) << 1) | (step >> 1))


def split_kernel(whole, pieces):
    share = pieces.shape[1] // COLUMN
    far = pieces.shape[1] // share
    for i, (h, b) in enumerate(NEAR_ORDER):
        starts = [((h * far + a) * QUAD + b) * share for a in range(far)]
        rows = [whole[start : start + share] for start in starts]
        pieces[i] = jnp.concatenate(rows, axis=0).astype(HALF)


def join_kernel(pieces, whole):
    share = pieces.shape[1] // COLUMN
    far = pieces.shape[1] // share
    parts = {key: pieces[i].astype(FULL) for i, key in enumerate(NEAR_ORDER)}
    for h in range(SIDES):
        for a in range(far):
            rows = [parts[h, b][a * share : (a + 1) * share] for b in range(QUAD)]
            start = (h * far + a) * QUAD * share
            whole[start : start + QUAD * share] = jnp.concatenate(rows, axis=0).astype(HALF)


def pack_kernel(lengths, features, cotangent, after, *packed):
    me = lax.axis_index("fsdp")
    place, y = me % QUAD, me // QUAD
    block = features.shape[1] // (COLUMN * QUAD)
    mine = lax.broadcasted_iota(jnp.int32, lengths.shape, 1) == me
    own = jnp.sum(jnp.where(mine, lengths[...].astype(FULL), 0.0), axis=1, keepdims=True)
    row = lax.broadcasted_iota(jnp.int32, cotangent.shape, 0).astype(FULL)
    masked = jnp.where(row < own, cotangent[...], jnp.zeros((), cotangent.dtype))
    for d in range(COLUMN):
        target = (y + d) % COLUMN
        for step in range(QUAD):
            source = pl.multiple_of((target * QUAD + block_of(place, step)) * block, block)
            packed[d][:, step * block : (step + 1) * block] = features[:, pl.ds(source, block)]
        packed[d][:, QUAD * block :] = masked


def sum_kernel(pieces, anchor, momentum, after, later, sums):
    total = pieces[0].astype(FULL)
    for i in range(1, NEAR):
        total += pieces[i].astype(FULL)
    base = anchor[...] - 0.7 * 0.9 * 0.9 * momentum[...]
    high = base.astype(HALF).astype(FULL)
    value = jnp.concatenate([total, high, base - high], axis=0).astype(HALF)
    for i in range(sums.shape[0]):
        sums[i] = value


def update_kernel(sums, anchor, momentum, anchor_out, momentum_out, fresh, delta):
    share = anchor.shape[0]
    far = sums.shape[0]
    near_rows = far * share
    parts = [sums[i].astype(FULL) for i in range(far)]
    total = parts[0][:near_rows]
    for part in parts[1:]:
        total += part[:near_rows]
    total = total / (NEAR * far)
    delta[...] = total
    place = lax.axis_index("replica") // QUAD % far
    own = delta[pl.ds(pl.multiple_of(place * share, share), share), :]
    moved = 0.9 * momentum[...] + own
    momentum_out[...] = moved
    anchor_out[...] = anchor[...] - 0.7 * (own + 0.9 * moved)
    parts = [parts[FAR_ORDER.index(a)][near_rows:] for a in range(far)]
    bases = [part[:share] + part[share:] for part in parts]
    value = (jnp.concatenate(bases, axis=0) - 0.7 * 1.9 * total).astype(HALF)
    for i in range(NEAR):
        fresh[i] = value


def input_kernel(factor, after, own, beside, across, *refs):
    cotangents, results = refs[:COLUMN], refs[COLUMN]
    y = lax.axis_index("fsdp") // QUAD
    tokens = cotangents[0].shape[0]
    block = own.shape[0]
    left = jnp.concatenate([ref[...] for ref in cotangents], axis=0)
    for step, right in enumerate((own[...], beside[...], across[:block], across[block:])):
        product = lax.dot_general(left, right, (((1,), (1,)), ((), ())), preferred_element_type=FULL)
        product = (product * factor).astype(HALF)
        for d in range(COLUMN):
            part = product[d * tokens : (d + 1) * tokens]
            results[(y + 2 * COLUMN - d - LEAD) % COLUMN, :, step * block : (step + 1) * block] = part


def weight_kernel(*refs):
    packed, (after, own, passed, sent) = refs[:COLUMN], refs[COLUMN:]
    rows, keys = own.shape

    def columns(start, size):
        return jnp.concatenate([ref[:, start : start + size] for ref in packed], axis=0)

    def term(start, size):
        return lax.dot_general(
            columns(start, size), right, (((0,), (0,)), ((), ())), preferred_element_type=FULL
        )

    right = columns(QUAD * rows, keys)
    sent[...] = term(2 * rows, 2 * rows).astype(HALF)
    own[...] = term(0, rows)
    passed[...] = term(rows, rows)


def unpack_kernel(*refs):
    pieces, result, done = refs
    place = lax.axis_index("fsdp") % QUAD
    block = result.shape[1] // (COLUMN * QUAD)
    copies = []
    for d in range(COLUMN):
        for step in range(QUAD):
            target = ((d + LEAD) % COLUMN * QUAD + block_of(place, step)) * block
            copies.append(
                pltpu.make_async_copy(
                    pieces.at[d, :, pl.ds(step * block, block)],
                    result.at[:, pl.ds(pl.multiple_of(target, block), block)],
                    done.at[d * QUAD + step],
                )
            )
    for copy in copies:
        copy.start()
    for copy in copies:
        copy.wait()


def whole(shape):
    return pl.BlockSpec(shape, lambda *_: (0,) * len(shape))


def call(kernel, outs, ins, in_specs=None, out_specs=None, flops=0, moved=1 << 20, scratch=(), grid=()):
    outs = [jax.ShapeDtypeStruct(shape, dtype) for shape, dtype in outs]
    return pl.pallas_call(
        kernel,
        grid=grid,
        out_shape=outs,
        in_specs=in_specs or [VMEM] * len(ins),
        out_specs=out_specs or [whole(out.shape) for out in outs],
        scratch_shapes=scratch,
        compiler_params=pltpu.CompilerParams(vmem_limit_bytes=48 << 20),
        cost_estimate=pl.CostEstimate(flops=flops, bytes_accessed=moved, transcendentals=0),
    )(*ins)


def local(
    activations, cotangent, master, moment_one, moment_two, lengths, pseudo_grad, anchor, momentum
):
    shards = lax.axis_size("fsdp")
    replicas = lax.axis_size("replica")
    tokens, width = activations.shape[1:]
    keys = cotangent.shape[2]
    share = anchor.shape[1]
    rows = master.shape[1]
    wide = width // COLUMN
    factor = 1.0 / math.sqrt(width)
    flops = 2 * COLUMN * tokens * wide * keys

    beside = [(f, f ^ 2) for f in range(shards)]
    across = [(f, f ^ 1) for f in range(shards)]
    up = [[(f, (f + QUAD * d) % shards) for f in range(shards)] for d in range(COLUMN)]
    columns = [[QUAD * ((y + LEAD) % COLUMN) + j for y in range(COLUMN)] for j in range(QUAD)]
    depth = replicas // SIDES
    outer = depth // QUAD
    near = [[depth * h + QUAD * a + b for h, b in NEAR_ORDER] for a in range(outer)]
    far = [[depth * h + QUAD * a + b for a in FAR_ORDER] for h in range(SIDES) for b in range(QUAD)]

    (pieces,) = call(split_kernel, [((NEAR, outer * share, keys), HALF)], (pseudo_grad[0, 0],))
    near_pieces = lax.all_to_all(pieces, "replica", 0, 0, axis_index_groups=near)

    packed = call(
        pack_kernel,
        [((tokens, wide + keys), HALF)] * COLUMN,
        (lengths, activations[0], cotangent[0], pieces),
        [VMEM, VMEM, VMEM, ANY],
        moved=3 << 20,
    )
    packed = [packed[0]] + [lax.ppermute(packed[d], "fsdp", up[d]) for d in (1, 2, 3)]

    raw = lax.optimization_barrier((master[0], packed[0]))[0]
    own = raw.astype(HALF)
    other = lax.ppermute(own, "fsdp", beside)

    (sums,) = call(
        sum_kernel,
        [((outer, (outer + 2) * share, keys), HALF)],
        (near_pieces, anchor[0], momentum[0], packed[0], other),
        [VMEM, VMEM, VMEM, ANY, ANY],
    )
    other = lax.optimization_barrier((other, sums, packed[1], packed[2], packed[3]))[0]
    both = lax.ppermute(jnp.concatenate([own, other], axis=0), "fsdp", across)
    sums = lax.all_to_all(sums, "replica", 0, 0, axis_index_groups=far)
    anchor_out, momentum_out, fresh = call(
        update_kernel,
        [((share, keys), FULL), ((share, keys), FULL), ((NEAR, outer * share, keys), HALF)],
        (sums, anchor[0], momentum[0]),
        scratch=[pltpu.VMEM((outer * share, keys), FULL)],
    )

    cot_spec = pl.BlockSpec((tokens, keys), lambda *_: (0, wide // keys))
    (products,) = call(
        lambda *refs: input_kernel(factor, *refs),
        [((COLUMN, tokens, wide), HALF)],
        (fresh, own, other, both, *packed),
        [ANY, whole(own.shape), whole(own.shape), whole(both.shape)] + [cot_spec] * COLUMN,
        flops=flops,
        moved=3 << 20,
        grid=(1,),
    )
    spread = lax.all_to_all(fresh, "replica", 0, 0, axis_index_groups=near)
    outgoing, spread = lax.optimization_barrier((products, spread))
    back = lax.all_to_all(outgoing, "fsdp", 0, 0, axis_index_groups=columns)
    (spread,) = call(join_kernel, [(pseudo_grad.shape[2:], HALF)], (spread,))

    grad_own, grad_passed, sent = call(
        weight_kernel,
        [((rows, keys), FULL), ((rows, keys), FULL), ((2 * rows, keys), HALF)],
        (*packed, products),
        [VMEM] * COLUMN + [ANY],
        flops=flops,
        moved=5 << 20,
    )
    crossed = lax.ppermute(sent, "fsdp", across)
    passed = lax.ppermute((grad_passed + crossed[rows:].astype(FULL)).astype(HALF), "fsdp", beside)
    summed = lax.optimization_barrier(grad_own + crossed[:rows].astype(FULL))
    passed = lax.optimization_barrier((passed, spread))[0]
    summed = summed + passed.astype(FULL)

    grad = summed * factor
    first = 0.9 * moment_one[0] + 0.1 * grad
    second = 0.95 * moment_two[0] + 0.05 * grad * grad
    master_out = master[0] * (1.0 - 0.1 * 0.1) - 0.1 * first / (jnp.sqrt(second) + 1e-08)

    (input_grad,) = call(
        unpack_kernel,
        [((tokens, width), HALF)],
        (back,),
        [ANY],
        [ANY],
        scratch=[pltpu.SemaphoreType.DMA((COLUMN * QUAD,))],
        moved=2 << 20,
    )
    return (
        input_grad[None], master_out[None], spread[None], anchor_out[None], momentum_out[None]
    )


def solution(mesh):
    placed = (
        P("replica", "fsdp", None),
        P("replica", "fsdp", None),
        P("replica", "fsdp", None),
        P("replica", "fsdp", None),
        P("replica", "fsdp", None),
        P("replica", None),
        P("replica", "fsdp", None, None),
        P("fsdp", "replica", None),
        P("fsdp", "replica", None),
    )
    return jax.shard_map(
        local,
        mesh=mesh,
        in_specs=placed,
        out_specs=(
            P("replica", "fsdp", None),
            P("replica", "fsdp", None),
            P("fsdp", None, None),
            P("fsdp", "replica", None),
            P("fsdp", "replica", None),
        ),
        check_vma=False,
    )
```
